32 devices in a mesh: seq: 8 (over y, x, core), grp: 4 (over z).
Axes of the slice: x: 2, y: 2, z: 4, core: 2. Of those that a mesh axis runs over, the one named last changes fastest.
Arguments:
- normed_hidden_input: bfloat16 [4096, 4096], P(('grp', 'seq')), may hold values from -6 to 6
- frozen_query_rows: bfloat16 [4096, 4096], P(('grp', 'seq')), may hold values from -16 to 16
- frozen_key_rows: bfloat16 [4096, 1024], P(('grp', 'seq')), may hold values from -16 to 16
- attention_output_gradient: bfloat16 [4096, 4096], P(('grp', 'seq')), may hold values from -0.15625 to 0.15625
- adapter_down_weight: bfloat16 [64, 64, 4096], P('grp', None, 'seq'), may hold values from -0.09375 to 0.09375
- adapter_up_weight: bfloat16 [64, 64, 1024], P('grp', 'seq'), may hold values from -0.75 to 0.75
- segment_adapter_index: int32 [4, 4], replicated, may hold values from 0 to 63, as said below
- segment_block_count: int32 [4, 4], replicated, may hold values from 1 to 4, 8 in all within a row
- adapter_row_index: int32 [64], replicated, may hold values from 0 to 63, as said below
Outputs:
- down_grad: float32 [64, 64, 4096], P('grp', None, 'seq')
- up_grad: float32 [64, 64, 1024], P('grp', 'seq')
The draws below stay inside these ranges and needn't reach their ends.
Inputs may be any that keep to these rules, and one draw needn't show every extreme that they name: A permutation: adapter a is held in row adapter_row_index[a] of adapter_down_weight and adapter_up_weight. `segment_adapter_index`: call rows g * 16 to (g + 1) * 16 - 1 of adapter_down_weight the rows of index g of grp. In each sequence at most 2 segments use adapters held in the rows of one index of grp, and in every sequence some index holds exactly 2 of them. Tenants may repeat within and across sequences. `segment_block_count`: each row sums to 8; in each row some segment has exactly 4 blocks.
All inputs are finite; a program needn't handle non-finite values.
Results may differ from the reference program's by a relative error of at most 0.0056.
Values may be sent and summed in bfloat16 or wider, within the bound.
A program may use at most 64 MiB of HBM per device.

```python
import math
import jax
import jax.numpy as jnp
import numpy as np
from jax import lax

MODEL_WIDTH = 4096
HEADS = 32
KV_HEADS = 8
HEAD_DIM = 128
ADAPTER_RANK = 64
BLOCK = 128
QROWS = 512
TOK_DEV = 128
ADAPT_GRP = 16
SEQLEN = 1024
TOKENS = 4096
ADAPTER_COUNT = 64
VALUE_WIDTH = 1024
SEGS = 4
MOSTBLK = 4
CAP = 2
N_SEQ = 8
N_GRP = 4


def draw_frozen_key_rows(key, part):
    base_key = jax.random.fold_in(key, 2)
    base = jnp.clip(jax.random.normal(base_key, (TOKENS, KV_HEADS * HEAD_DIM)), -6.0, 6.0)
    return base.astype(jnp.bfloat16)


def draw_frozen_query_rows(key, part):
    base_key = jax.random.fold_in(key, 1)
    base = jnp.clip(jax.random.normal(base_key, (TOKENS, HEADS * HEAD_DIM)), -6.0, 6.0)
    return base.astype(jnp.bfloat16)


def tenant_layout(key):
    groups = ADAPTER_COUNT // ADAPT_GRP
    owner = jax.random.permutation(jax.random.fold_in(key, 31), ADAPTER_COUNT).astype(jnp.int32)
    inverse = jnp.zeros((ADAPTER_COUNT,), jnp.int32).at[owner].set(jnp.arange(ADAPTER_COUNT, dtype=jnp.int32))

    def one_sequence(seq_key):
        full_key, order_key, shuffle_key, local_key = jax.random.split(seq_key, 4)
        full_group = jax.random.randint(full_key, (), 0, groups)
        pool = jnp.arange(groups * CAP, dtype=jnp.int32) // CAP
        scores = jax.random.permutation(order_key, groups * CAP).astype(jnp.int32)
        scores = jnp.where(pool == full_group, -1, scores)
        picked = pool[jnp.argsort(scores, stable=True)[:SEGS]]
        picked = picked[jax.random.permutation(shuffle_key, SEGS)]
        slots = picked * ADAPT_GRP + jax.random.randint(local_key, (SEGS,), 0, ADAPT_GRP)
        return inverse[slots]
    seq_keys = jax.random.split(jax.random.fold_in(key, 32), groups)
    tenants = jax.vmap(one_sequence)(seq_keys).astype(jnp.int32)
    return (owner, tenants)


def draw_adapter_row_index(key, part):
    owner, tenants = tenant_layout(key)
    return owner


def draw_segment_adapter_index(key, part):
    owner, tenants = tenant_layout(key)
    return tenants


def block_scale(stream_key, shape, cuts, low, largest):
    loudness, own = 1.0, jax.random.fold_in(stream_key, 6)
    for dim, blocks in cuts:
        steps = jnp.exp(jax.random.uniform(jax.random.fold_in(own, dim), (blocks,), jnp.float32, low / len(cuts), largest / len(cuts)))
        loudness = loudness * jnp.repeat(steps, shape[dim] // blocks).reshape([-1 if axis == dim else 1 for axis in range(len(shape))])
    return loudness


def split_up(count, total, most, skew):
    loads = [(1 << 20) // math.isqrt(grade ** skew) + 1 for grade in range(2, count + 1)]
    spare, given = total - most - (count - 1), [1] * (count - 1)
    while spare > 0:
        candidates = [i for i in range(count - 1) if given[i] < most]
        whole, remaining = sum([loads[i] for i in candidates]), spare
        for i in candidates:
            extra = min(most - given[i], max(1, remaining * loads[i] // whole), spare)
            given[i] = given[i] + extra
            spare = spare - extra
    return np.array([most] + given)


def ragged_sizes(own_key, number_of, total, limit, slope):
    if number_of == 2:
        one = jax.random.randint(own_key, (), max(1, total - limit), min(limit, total - 1) + 1)
        return jnp.stack([one, total - one])
    lengths = jnp.asarray(split_up(number_of, total, limit, slope), jnp.int32)
    pairs = (number_of - 1) // 2
    donor, receiver = lengths[1:1 + 2 * pairs:2], lengths[2:2 + 2 * pairs:2]
    slack = jnp.minimum(donor - 1, limit - receiver)
    moved = jax.random.randint(jax.random.fold_in(own_key, 1), (pairs,), 0, 1 << 20) % (slack + 1)
    lengths = lengths.at[1:1 + 2 * pairs:2].set(donor - moved).at[2:2 + 2 * pairs:2].set(receiver + moved)
    return lengths[jax.random.permutation(jax.random.fold_in(own_key, 2), number_of)]


def noise(key, shape, deviation, bound, pieces=(), held_as=jnp.bfloat16):
    array = deviation * jax.random.normal(key, shape, jnp.float32)
    if pieces:
        array = array * block_scale(key, shape, pieces, -0.22, 0.18)
    return jnp.clip(array, -bound, bound).astype(held_as)


def setup_inputs(seed: int = 0) -> dict:
    key_list = jax.random.split(jax.random.key(seed), 10)
    normed_hidden_input = noise(key_list[0], (TOKENS, MODEL_WIDTH), 1.0, 6.0, ((0, 32),))
    frozen_query_rows = draw_frozen_query_rows(jax.random.fold_in(key_list[9], 71), 0)
    frozen_key_rows = draw_frozen_key_rows(jax.random.fold_in(key_list[9], 71), 0)
    attention_output_gradient = noise(key_list[3], (TOKENS, HEADS * HEAD_DIM), 0.01, 0.15625, ((0, 32),))
    adapter_down_weight = noise(key_list[4], (ADAPTER_COUNT, ADAPTER_RANK, MODEL_WIDTH), MODEL_WIDTH ** -0.5, 0.09375, ((0, 4), (2, 8)))
    adapter_up_weight = noise(key_list[5], (ADAPTER_COUNT, ADAPTER_RANK, VALUE_WIDTH), ADAPTER_RANK ** -0.5, 0.75, ((0, 4), (1, 8)))
    segment_adapter_index = draw_segment_adapter_index(jax.random.fold_in(key_list[9], 71), 0)
    segment_block_count = jax.vmap(lambda own: ragged_sizes(own, SEGS, N_SEQ * TOK_DEV // BLOCK, MOSTBLK, 2))(jax.random.split(key_list[7], N_GRP)).reshape((N_GRP, SEGS)).astype(jnp.int32)
    adapter_row_index = draw_adapter_row_index(jax.random.fold_in(key_list[9], 71), 0)
    return {"normed_hidden_input": normed_hidden_input, "frozen_query_rows": frozen_query_rows, "frozen_key_rows": frozen_key_rows, "attention_output_gradient": attention_output_gradient, "adapter_down_weight": adapter_down_weight, "adapter_up_weight": adapter_up_weight, "segment_adapter_index": segment_adapter_index, "segment_block_count": segment_block_count, "adapter_row_index": adapter_row_index}


adapter_scale = 2.0

def attend_head(query_head, key_head, grad_head, segment_ids, query_rows, reach):
    length, head_width = query_head.shape
    padded_keys = jnp.concatenate([jnp.zeros((reach, head_width), key_head.dtype), key_head], 0)
    padded_ids = jnp.concatenate([jnp.full((reach,), -1, jnp.int32), segment_ids.astype(jnp.int32)], 0)
    window = query_rows + reach
    factor = 1.0 / math.sqrt(head_width)

    def one_block(totals, number):
        offset = number * query_rows
        query_block = lax.dynamic_slice_in_dim(query_head, offset, query_rows, 0)
        grad_block = lax.dynamic_slice_in_dim(grad_head, offset, query_rows, 0)
        key_block = lax.dynamic_slice_in_dim(padded_keys, offset, window, 0)
        key_ids = lax.dynamic_slice_in_dim(padded_ids, offset, window, 0)
        query_ids = lax.dynamic_slice_in_dim(segment_ids.astype(jnp.int32), offset, query_rows, 0)
        scores = jnp.dot(query_block, key_block.T, preferred_element_type=jnp.float32) * factor
        query_pos = offset + jnp.arange(query_rows, dtype=jnp.int32)
        key_pos = offset - reach + jnp.arange(window, dtype=jnp.int32)
        allowed = (key_ids[None, :] == query_ids[:, None]) & (key_pos[None, :] <= query_pos[:, None])
        scores = jnp.where(allowed, scores, jnp.float32(-1e+30))
        highest = lax.optimization_barrier(jnp.max(scores, axis=1, keepdims=True))
        expo = jnp.exp(scores - highest)
        probabilities = (expo / lax.optimization_barrier(jnp.sum(expo, axis=1, keepdims=True))).astype(jnp.bfloat16)
        contribution = jnp.dot(probabilities.T, grad_block, preferred_element_type=jnp.float32)
        current = lax.dynamic_slice_in_dim(totals, offset, window, 0)
        totals = lax.dynamic_update_slice_in_dim(totals, current + contribution, offset, 0)
        return (totals, None)
    initial = jnp.zeros((length + reach, head_width), jnp.float32)
    totals, _ = lax.scan(one_block, initial, jnp.arange(length // query_rows, dtype=jnp.int32))
    return totals[reach:].astype(jnp.bfloat16)

def block_segment(blocks_row, amount):
    ends = jnp.cumsum(blocks_row)
    return lax.optimization_barrier(jnp.sum((jnp.arange(amount, dtype=jnp.int32)[:, None] >= ends[None, :]).astype(jnp.int32), axis=1))

def reference(normed_hidden_input, frozen_query_rows, frozen_key_rows, attention_output_gradient, adapter_down_weight, adapter_up_weight, segment_adapter_index, segment_block_count, adapter_row_index):
    block_total = SEQLEN // BLOCK
    reach = MOSTBLK * BLOCK
    group_size = HEADS // KV_HEADS

    def one_sequence(running, number):
        down_totals, up_totals = running
        offset = number * SEQLEN
        seq_hidden = lax.dynamic_slice_in_dim(normed_hidden_input, offset, SEQLEN, 0)
        seq_queries = lax.dynamic_slice_in_dim(frozen_query_rows, offset, SEQLEN, 0)
        seq_keys = lax.dynamic_slice_in_dim(frozen_key_rows, offset, SEQLEN, 0)
        seq_grads = lax.dynamic_slice_in_dim(attention_output_gradient, offset, SEQLEN, 0)
        segment_of_block = block_segment(segment_block_count[number], block_total)
        tenant_of_block = segment_adapter_index[number][segment_of_block]
        block_slot_index = adapter_row_index[tenant_of_block].astype(jnp.int32)
        segment_ids = jnp.broadcast_to(segment_of_block[:, None], (block_total, BLOCK)).reshape(SEQLEN)
        down_weight_blocks = adapter_down_weight[block_slot_index]
        up_weight_blocks = adapter_up_weight[block_slot_index]
        hidden_input_blocks = seq_hidden.reshape(block_total, BLOCK, MODEL_WIDTH)
        reduced_rank_part = jnp.einsum('jyw,jaw->jya', hidden_input_blocks.astype(jnp.float32), down_weight_blocks.astype(jnp.float32)).astype(jnp.bfloat16)
        query_heads = jnp.transpose(seq_queries.reshape(SEQLEN, HEADS, HEAD_DIM), (1, 0, 2))
        key_heads = jnp.transpose(jnp.repeat(seq_keys.reshape(SEQLEN, KV_HEADS, HEAD_DIM), group_size, axis=1), (1, 0, 2))
        grad_heads = jnp.transpose(seq_grads.reshape(SEQLEN, HEADS, HEAD_DIM), (1, 0, 2))

        def per_head(triple):
            return attend_head(triple[0], triple[1], triple[2], segment_ids, QROWS, reach)
        head_grad = lax.map(per_head, (query_heads, key_heads, grad_heads))
        value_grad = lax.optimization_barrier(jnp.sum(head_grad.reshape(KV_HEADS, group_size, SEQLEN, HEAD_DIM), axis=1, dtype=jnp.float32))
        value_grad = jnp.transpose(value_grad, (1, 0, 2)).reshape(SEQLEN, VALUE_WIDTH).astype(jnp.bfloat16)
        value_row_blocks = value_grad.reshape(block_total, BLOCK, VALUE_WIDTH)
        up_weight_terms = adapter_scale * jnp.einsum('fvg,fvn->fgn', reduced_rank_part.astype(jnp.float32), value_row_blocks.astype(jnp.float32))
        backward_rank_part = (adapter_scale * jnp.einsum('vaw,vpw->vap', value_row_blocks.astype(jnp.float32), up_weight_blocks.astype(jnp.float32))).astype(jnp.bfloat16)
        down_weight_terms = jnp.einsum('jcy,jct->jyt', backward_rank_part.astype(jnp.float32), hidden_input_blocks.astype(jnp.float32))
        down_totals = down_totals.at[block_slot_index].add(down_weight_terms)
        up_totals = up_totals.at[block_slot_index].add(up_weight_terms)
        return ((down_totals, up_totals), None)
    initial = (jnp.zeros((ADAPTER_COUNT, ADAPTER_RANK, MODEL_WIDTH), jnp.float32), jnp.zeros((ADAPTER_COUNT, ADAPTER_RANK, VALUE_WIDTH), jnp.float32))
    (down_totals, up_totals), _ = lax.scan(one_sequence, initial, jnp.arange(N_GRP, dtype=jnp.int32))
    return (down_totals, up_totals)
```

```python
import functools
import math

import jax
import jax.numpy as jnp
from jax import lax
from jax.experimental import pallas as pl
from jax.experimental.pallas import tpu as pltpu
from jax.sharding import PartitionSpec as P

HEAD_DIM = 128
BLOCK = 128
SCALE = 2.0
MESH = pl.DeviceIdType.MESH
F32 = jnp.float32
BF16 = jnp.bfloat16


def segment_places(sai, row, seq, segs, resident, cap):
    owners, places, locals_ = [], [], []
    ranks = []
    for j in range(segs):
        slot = row[sai[seq, j]]
        owner = slot // resident
        rank = jnp.int32(0)
        for i in range(j):
            rank = rank + jnp.where(owners[i] == owner, 1, 0)
        owners.append(owner)
        ranks.append(rank)
        places.append(owner * cap + rank)
        locals_.append(slot - owner * resident)
    return owners, ranks, places, locals_


def chosen_rows(sai, row, group, sel, groups, segs, resident, cap, empty):
    def one(seq, carry):
        owners, ranks, _, held = segment_places(sai, row, seq, segs, resident, cap)
        for c in range(cap):
            value = jnp.int32(empty)
            for j in range(segs):
                value = jnp.where((owners[j] == group) & (ranks[j] == c), held[j], value)
            sel[seq * cap + c] = value
        return carry

    lax.fori_loop(0, groups, one, 0)


def exchange_kernel(
    cfg, sai, cnt, row, x, q, k, o, ad, au, down_out, up_out,
    seg_s, place_s, sel_s,
    qb, ob, kb, xb, adv, auv, asend, usend, acand, ucand, u2send, u2, uf,
    lowsend, lowr, vgsend, vgr, blr, utsend, utr, dsend, tf, tsend, acc,
    seq_send, seq_recv, grp_send, grp_recv, near,
):
    n, groups, cap, segs, resident, rank, rp, fw, hh, gs, reach, pad = cfg
    s = lax.axis_index("seq")
    g = lax.axis_index("grp")
    hw = hh * HEAD_DIM
    blk = BLOCK

    def lanes(index, width):
        return pl.ds(pl.multiple_of(index * width, 128), width)

    def seq_copy(kind, src, dst, peer, origin):
        return pltpu.make_async_remote_copy(
            src_ref=src, dst_ref=dst, send_sem=seq_send.at[kind, peer],
            recv_sem=seq_recv.at[kind, origin], device_id={"seq": peer}, device_id_type=MESH)

    def grp_copy(kind, src, dst, peer, origin):
        return pltpu.make_async_remote_copy(
            src_ref=src, dst_ref=dst, send_sem=grp_send.at[kind, peer],
            recv_sem=grp_recv.at[kind, origin], device_id={"grp": peer}, device_id_type=MESH)

    def key_src(p):
        return k.at[:, lanes((p * hh) // gs, HEAD_DIM)]

    seq_kinds = {
        "k": (0, key_src, lambda i: kb.at[pad + i]),
        "q": (1, lambda p: q.at[:, lanes(p, hw)], lambda i: qb.at[i]),
        "o": (2, lambda p: o.at[:, lanes(p, hw)], lambda i: ob.at[i]),
        "x": (3, lambda p: x.at[:, lanes(p, fw)], lambda i: xb.at[i]),
        "u": (4, lambda p: u2send.at[p], lambda i: u2.at[i]),
        "low": (5, lambda p: lowsend.at[p], lambda i: lowr.at[i]),
        "vg": (6, lambda p: vgsend.at[p], lambda i: vgr.at[i]),
        "bl": (7, lambda p: blr.at[s], lambda i: blr.at[i]),
        "ut": (8, lambda p: utsend.at[p], lambda i: utr.at[i]),
    }
    grp_kinds = {
        "a": (0, lambda p: asend.at[pl.ds(p * cap, cap)], lambda i: acand.at[pl.ds(i * cap, cap)]),
        "b": (1, lambda p: usend.at[pl.ds(p * cap, cap)], lambda i: ucand.at[pl.ds(i * cap, cap)]),
        "d": (2, lambda p: dsend.at[p], lambda i: down_out.at[i]),
        "t": (3, lambda p: tsend.at[p], lambda i: up_out.at[i]),
    }

    def send_one(name, peer):
        kind, src, dst = seq_kinds[name]
        seq_copy(kind, src(peer), dst(s), peer, s).start()

    def wait_one(name, origin):
        kind, src, dst = seq_kinds[name]
        seq_copy(kind, src(origin), dst(origin), origin, origin).wait_recv()

    def each_peer(fn, me, count):
        def body(step, carry):
            fn(lax.rem(me + step, count))
            return carry
        lax.fori_loop(1, count, body, 0)

    def send_seq(name):
        each_peer(lambda p: send_one(name, p), s, n)

    def wait_seq(name):
        each_peer(lambda p: wait_one(name, p), s, n)

    def sent_seq(name):
        kind, src, dst = seq_kinds[name]
        each_peer(lambda p: seq_copy(kind, src(p), dst(s), p, s).wait_send(), s, n)

    def send_grp_one(name, peer):
        kind, src, dst = grp_kinds[name]
        grp_copy(kind, src(peer), dst(g), peer, g).start()

    def wait_grp(name):
        kind, src, dst = grp_kinds[name]
        each_peer(lambda p: grp_copy(kind, src(p), dst(p), p, p).wait_recv(), g, groups)

    def sent_grp(name):
        kind, src, dst = grp_kinds[name]
        each_peer(lambda p: grp_copy(kind, src(p), dst(g), p, g).wait_send(), g, groups)

    barrier = pltpu.get_barrier_semaphore()

    def greet_seq(p):
        pl.semaphore_signal(barrier, inc=1, device_id={"seq": p}, device_id_type=MESH)

    def greet_grp(p):
        pl.semaphore_signal(barrier, inc=1, device_id={"grp": p}, device_id_type=MESH)

    each_peer(greet_seq, s, n)
    each_peer(greet_grp, g, groups)

    own = {}
    for number, name in enumerate(("k", "q", "o", "x")):
        _, src, dst = seq_kinds[name]
        own[name] = pltpu.make_async_copy(src(s), dst(s), near.at[number])
    own["a"] = pltpu.make_async_copy(ad, adv, near.at[4])
    own["b"] = pltpu.make_async_copy(au, auv, near.at[5])
    for name in ("a", "b", "k", "q", "o", "x"):
        own[name].start()

    chosen_rows(sai, row, g, sel_s, groups, segs, resident, cap, 0)
    owners, ranks, places, _ = segment_places(sai, row, g, segs, resident, cap)
    ends = []
    total = jnp.int32(0)
    for j in range(segs):
        total = total + cnt[g, j]
        ends.append(total)
    for b in range(pad):
        seg_s[b] = jnp.int32(-1)

    def one_block(b, carry):
        seg = jnp.int32(0)
        for j in range(segs):
            seg = seg + jnp.where(b >= ends[j], 1, 0)
        place = jnp.int32(0)
        for j in range(segs):
            place = jnp.where(seg == j, places[j], place)
        seg_s[pad + b] = seg
        place_s[b] = place
        return carry

    lax.fori_loop(0, n, one_block, 0)

    pl.semaphore_wait(barrier, n - 1 + groups - 1)
    send_seq("k")
    for_heads = ("q", "o")

    def send_heads(p):
        for name in for_heads:
            send_one(name, p)

    each_peer(send_heads, s, n)

    own["a"].wait()
    own["b"].wait()

    def pick(slot, carry):
        index = sel_s[slot]
        asend[slot] = adv[index]
        usend[slot] = auv[index]
        return carry

    lax.fori_loop(0, groups * cap, pick, 0)
    each_peer(lambda p: send_grp_one("b", p), g, groups)
    each_peer(lambda p: send_grp_one("a", p), g, groups)
    send_seq("x")
    for c in range(cap):
        acand[g * cap + c] = asend[g * cap + c]
        ucand[g * cap + c] = usend[g * cap + c]
    for b in range(pad):
        kb[b] = jnp.zeros_like(kb[b])
    acc[...] = jnp.zeros_like(acc)

    wait_grp("b")

    def route(b, carry):
        u2send[b] = ucand[place_s[b]]
        return carry

    lax.fori_loop(0, n, route, 0)
    send_seq("u")
    u2[s] = u2send[s]

    factor = math.log2(math.e) / math.sqrt(HEAD_DIM)

    def attend(b, first, count):
        width = count * blk
        queries = jnp.concatenate(
            [qb[b, :, h * HEAD_DIM:(h + 1) * HEAD_DIM] for h in range(hh)], 0)
        grads = jnp.concatenate(
            [ob[b, :, h * HEAD_DIM:(h + 1) * HEAD_DIM] for h in range(hh)], 0)
        keys = kb[pl.ds(first, count)].reshape(width, HEAD_DIM)
        scores = lax.dot_general(queries, keys, (((1,), (1,)), ((), ())),
                                 preferred_element_type=F32)
        column = lax.broadcasted_iota(jnp.int32, (1, width), 1)
        ids = jnp.full((1, width), seg_s[first], jnp.int32)
        for j in range(1, count):
            ids = jnp.where(column >= j * blk, seg_s[first + j], ids)
        rows = lax.broadcasted_iota(jnp.int32, (blk, width), 0)
        columns = lax.broadcasted_iota(jnp.int32, (blk, width), 1)
        seen = (ids == seg_s[pad + b]) & (columns - (count - 1) * blk <= rows)
        bias = jnp.where(seen, F32(0), F32(-1e30))
        scores = (scores.reshape(hh, blk, width) + bias[None]).reshape(hh * blk, width)
        highest = jnp.max(scores, axis=1, keepdims=True)
        expo = jnp.exp2((scores - highest) * factor)
        probs = (expo * (1.0 / jnp.sum(expo, axis=1, keepdims=True))).astype(BF16)
        part = lax.dot_general(probs, grads, (((0,), (0,)), ((), ())),
                               preferred_element_type=F32)
        acc[pl.ds(first, count)] += part.reshape(count, blk, HEAD_DIM)

    def arrived(b):
        @pl.when(b != s)
        def _():
            for name in ("k", "q", "o"):
                wait_one(name, b)

        @pl.when(b == s)
        def _():
            for name in ("k", "q", "o"):
                own[name].wait()

    def finish(b):
        vgsend[b] = acc[pad + b].astype(BF16)

        @pl.when(b != s)
        def _():
            send_one("vg", b)

        @pl.when(b == s)
        def _():
            vgr[s] = vgsend[b]

    if pad == 0:
        for b in range(n):
            arrived(b)
            attend(b, max(b - reach + 1, 0), min(b + 1, reach))
            if b >= reach - 1:
                finish(b - reach + 1)
        for b in range(n - reach + 1, n):
            finish(b)
    else:
        def step(b, carry):
            arrived(b)
            attend(b, b, reach)
            return carry

        lax.fori_loop(0, n, step, 0)

        def last(b, carry):
            finish(b)
            return carry

        lax.fori_loop(0, n, last, 0)

    wait_seq("u")
    for i in range(n):
        uf[i * rp:(i + 1) * rp, :] = u2[i].astype(F32)
    up_rows = uf[...].astype(BF16)
    wait_seq("vg")
    share = gs // hh
    heads = []
    for kv in range(n // share):
        if share == 1:
            heads.append(vgr[kv])
        else:
            whole = vgr[kv * share].astype(F32)
            for i in range(1, share):
                whole = whole + vgr[kv * share + i].astype(F32)
            heads.append(whole.astype(BF16))
    value_grad = jnp.concatenate(heads, 1)
    back = SCALE * lax.dot_general(up_rows, value_grad, (((1,), (1,)), ((), ())),
                                   preferred_element_type=F32)
    blr[s] = back.astype(BF16)
    send_seq("bl")

    wait_grp("a")
    own["x"].wait()
    wait_seq("x")

    def lowered(b, carry):
        lowsend[b] = lax.dot_general(acand[place_s[b]], xb[b], (((1,), (1,)), ((), ())),
                                     preferred_element_type=F32)
        return carry

    lax.fori_loop(0, n, lowered, 0)
    send_seq("low")
    lowr[s] = lowsend[s]

    wait_seq("bl")
    features = xb[...].reshape(n * blk, fw)

    def down_terms(peer):
        rows = []
        for c in range(cap):
            rows.append(jnp.concatenate(
                [jnp.where(place_s[b] == peer * cap + c, blr[b].astype(F32), F32(0)).astype(BF16)
                 for b in range(n)], 1))
        dsend[peer] = lax.dot_general(jnp.concatenate(rows, 0), features,
                                      (((1,), (0,)), ((), ())),
                                      preferred_element_type=F32).astype(BF16)

    def down_send(peer):
        down_terms(peer)
        send_grp_one("d", peer)

    each_peer(down_send, g, groups)
    down_terms(g)
    mine_down = pltpu.make_async_copy(dsend.at[g], down_out.at[g], near.at[6])
    mine_down.start()

    wait_seq("low")
    low = lowr[0]
    for i in range(1, n):
        low = low + lowr[i]
    terms = SCALE * lax.dot_general(low.astype(BF16), value_grad, (((1,), (0,)), ((), ())),
                                    preferred_element_type=F32)
    for i in range(n):
        utsend[i] = terms[i * rp:(i + 1) * rp, :]
    send_seq("ut")
    utr[s] = utsend[s]
    wait_seq("ut")

    def up_terms(peer):
        for c in range(cap):
            def add(b, total):
                return total + jnp.where(place_s[b] == peer * cap + c, utr[b], F32(0))
            tf[c * rp:(c + 1) * rp, :] = lax.fori_loop(
                0, n, add, jnp.zeros(utr.shape[1:], F32))
        tsend[peer] = tf[...].astype(BF16)

    def up_send(peer):
        up_terms(peer)
        send_grp_one("t", peer)

    each_peer(up_send, g, groups)
    up_terms(g)
    mine_up = pltpu.make_async_copy(tsend.at[g], up_out.at[g], near.at[7])
    mine_up.start()

    for name in seq_kinds:
        sent_seq(name)
    for name in grp_kinds:
        sent_grp(name)
    mine_down.wait()
    mine_up.wait()
    wait_grp("d")
    wait_grp("t")


def spread_kernel(cfg, sai, row, down, up, down_grad, up_grad, sel_s):
    groups, cap, segs, resident, rank, rp = cfg
    step = pl.program_id(0)
    here = down_grad.shape[0]
    g = lax.axis_index("grp")

    @pl.when(step == 0)
    def _():
        chosen_rows(sai, row, g, sel_s, groups, segs, resident, cap, -1)

    def rows_of(terms, ranks):
        count = groups * cap
        slots = lax.broadcasted_iota(jnp.int32, (1, count * ranks), 1)
        target = jnp.full((1, count * ranks), -1, jnp.int32)
        for i in range(count):
            inside = (slots >= i * ranks) & (slots < (i + 1) * ranks)
            first = jnp.where(sel_s[i] < 0, -(1 << 20), (sel_s[i] - step * here) * ranks)
            target = jnp.where(inside, first + slots - i * ranks, target)
        rows = lax.broadcasted_iota(jnp.int32, (here * ranks, count * ranks), 0)
        onehot = jnp.where(rows == target, F32(1), F32(0)).astype(BF16)
        return lax.dot_general(onehot, terms, (((1,), (0,)), ((), ())), preferred_element_type=F32)

    down_grad[...] = rows_of(down[...], rank).reshape(down_grad.shape)
    up_grad[...] = rows_of(up[...], rp).reshape(up_grad.shape)


def local(x, q, k, o, ad, au, sai, cnt, row):
    groups = lax.axis_size("grp")
    n = lax.axis_size("seq")
    tokens = x.shape[0]
    fw = ad.shape[2]
    resident, rank = ad.shape[0], ad.shape[1]
    rp, vw = au.shape[1], au.shape[2]
    segs = sai.shape[1]
    cap = max(2, (segs + groups - 1) // groups)
    reach = min(16, n * tokens // (2 * BLOCK))
    heads = q.shape[1] // HEAD_DIM
    hh = heads // n
    gs = heads // (vw // HEAD_DIM)
    assert tokens == BLOCK and gs % hh == 0
    pad = 0 if n <= 8 else reach - 1
    cfg = (n, groups, cap, segs, resident, rank, rp, fw, hh, gs, reach, pad)
    slots = groups * cap
    smem = pl.BlockSpec(memory_space=pltpu.SMEM)
    hbm = pl.BlockSpec(memory_space=pl.ANY)
    down, up = pl.pallas_call(
        functools.partial(exchange_kernel, cfg),
        out_shape=(
            jax.ShapeDtypeStruct((groups, cap * rank, fw), BF16),
            jax.ShapeDtypeStruct((groups, cap * rp, vw), BF16),
        ),
        in_specs=[smem] * 3 + [hbm] * 6,
        out_specs=(hbm, hbm),
        scratch_shapes=[
            pltpu.SMEM((n + pad,), jnp.int32),
            pltpu.SMEM((n,), jnp.int32),
            pltpu.SMEM((slots,), jnp.int32),
            pltpu.VMEM((n, BLOCK, hh * HEAD_DIM), BF16),
            pltpu.VMEM((n, BLOCK, hh * HEAD_DIM), BF16),
            pltpu.VMEM((n + pad, BLOCK, HEAD_DIM), BF16),
            pltpu.VMEM((n, BLOCK, fw), BF16),
            pltpu.VMEM(ad.shape, BF16),
            pltpu.VMEM(au.shape, BF16),
            pltpu.VMEM((slots, rank, fw), BF16),
            pltpu.VMEM((slots, rp, vw), BF16),
            pltpu.VMEM((slots, rank, fw), BF16),
            pltpu.VMEM((slots, rp, vw), BF16),
            pltpu.VMEM((n, rp, vw), BF16),
            pltpu.VMEM((n, rp, vw), BF16),
            pltpu.VMEM((rank, vw), F32),
            pltpu.VMEM((n, rank, BLOCK), F32),
            pltpu.VMEM((n, rank, BLOCK), F32),
            pltpu.VMEM((n, BLOCK, HEAD_DIM), BF16),
            pltpu.VMEM((n, BLOCK, HEAD_DIM), BF16),
            pltpu.VMEM((n, rank, BLOCK), BF16),
            pltpu.VMEM((n, rp, vw), F32),
            pltpu.VMEM((n, rp, vw), F32),
            pltpu.VMEM((groups, cap * rank, fw), BF16),
            pltpu.VMEM((cap * rp, vw), F32),
            pltpu.VMEM((groups, cap * rp, vw), BF16),
            pltpu.VMEM((n + pad, BLOCK, HEAD_DIM), F32),
            pltpu.SemaphoreType.DMA((9, n)),
            pltpu.SemaphoreType.DMA((9, n)),
            pltpu.SemaphoreType.DMA((4, groups)),
            pltpu.SemaphoreType.DMA((4, groups)),
            pltpu.SemaphoreType.DMA((8,)),
        ],
        compiler_params=pltpu.CompilerParams(
            collective_id=0, has_side_effects=True, vmem_limit_bytes=40 * 1024 * 1024),
        name="exchange",
    )(sai, cnt, row, x, q, k, o, ad, au)
    steps = 4
    here = resident // steps
    return pl.pallas_call(
        functools.partial(spread_kernel, (groups, cap, segs, resident, rank, rp)),
        grid=(steps,),
        out_shape=(
            jax.ShapeDtypeStruct((resident, rank, fw), F32),
            jax.ShapeDtypeStruct((resident, rp, vw), F32),
        ),
        in_specs=[
            smem, smem,
            pl.BlockSpec((slots * rank, fw), lambda i: (0, 0)),
            pl.BlockSpec((slots * rp, vw), lambda i: (0, 0)),
        ],
        out_specs=(
            pl.BlockSpec((here, rank, fw), lambda i: (i, 0, 0)),
            pl.BlockSpec((here, rp, vw), lambda i: (i, 0, 0)),
        ),
        scratch_shapes=[pltpu.SMEM((slots,), jnp.int32)],
        compiler_params=pltpu.CompilerParams(vmem_limit_bytes=40 * 1024 * 1024),
        name="spread",
    )(sai, row, down.reshape(slots * rank, fw), up.reshape(slots * rp, vw))


def solution(mesh):
    return jax.shard_map(
        local,
        mesh=mesh,
        in_specs=(
            P(("grp", "seq"), None),
            P(("grp", "seq"), None),
            P(("grp", "seq"), None),
            P(("grp", "seq"), None),
            P("grp", None, "seq"),
            P("grp", "seq", None),
            P(),
            P(),
            P(),
        ),
        out_specs=(P("grp", None, "seq"), P("grp", "seq", None)),
        check_vma=False,
    )
```

```python
import functools
import math

import jax
import jax.numpy as jnp
from jax import lax
from jax.experimental import pallas as pl
from jax.experimental.pallas import tpu as pltpu
from jax.sharding import PartitionSpec as P

HEAD_DIM = 128
BLOCK = 128
SCALE = 2.0
MESH = pl.DeviceIdType.MESH
F32 = jnp.float32
BF16 = jnp.bfloat16


def segment_places(sai, row, seq, segs, resident, cap):
    owners, places, locals_ = [], [], []
    ranks = []
    for j in range(segs):
        slot = row[sai[seq, j]]
        owner = slot // resident
        rank = jnp.int32(0)
        for i in range(j):
            rank = rank + jnp.where(owners[i] == owner, 1, 0)
        owners.append(owner)
        ranks.append(rank)
        places.append(owner * cap + rank)
        locals_.append(slot - owner * resident)
    return owners, ranks, places, locals_


def chosen_rows(sai, row, group, sel, groups, segs, resident, cap, empty):
    def one(seq, carry):
        owners, ranks, _, held = segment_places(sai, row, seq, segs, resident, cap)
        for c in range(cap):
            value = jnp.int32(empty)
            for j in range(segs):
                value = jnp.where((owners[j] == group) & (ranks[j] == c), held[j], value)
            sel[seq * cap + c] = value
        return carry

    lax.fori_loop(0, groups, one, 0)


def exchange_kernel(
    cfg, sai, cnt, row, x, q, k, o, ad, au, down_out, up_out,
    seg_s, place_s, sel_s,
    qb, ob, kb, xb, adv, auv, asend, usend, acand, ucand, u2send, u2, uf,
    lowsend, lowr, vgsend, vgr, blr, utsend, utr, dsend, tf, tsend, acc,
    seq_send, seq_recv, grp_send, grp_recv, near,
):
    n, groups, cap, segs, resident, rank, rp, fw, hh, gs, reach, pad = cfg
    s = lax.axis_index("seq")
    g = lax.axis_index("grp")
    hw = hh * HEAD_DIM
    blk = BLOCK

    def lanes(index, width):
        return pl.ds(pl.multiple_of(index * width, 128), width)

    def seq_copy(kind, src, dst, peer, origin):
        return pltpu.make_async_remote_copy(
            src_ref=src, dst_ref=dst, send_sem=seq_send.at[kind, peer],
            recv_sem=seq_recv.at[kind, origin], device_id={"seq": peer}, device_id_type=MESH)

    def grp_copy(kind, src, dst, peer, origin):
        return pltpu.make_async_remote_copy(
            src_ref=src, dst_ref=dst, send_sem=grp_send.at[kind, peer],
            recv_sem=grp_recv.at[kind, origin], device_id={"grp": peer}, device_id_type=MESH)

    def key_src(p):
        return k.at[:, lanes((p * hh) // gs, HEAD_DIM)]

    seq_kinds = {
        "k": (0, key_src, lambda i: kb.at[pad + i]),
        "q": (1, lambda p: q.at[:, lanes(p, hw)], lambda i: qb.at[i]),
        "o": (2, lambda p: o.at[:, lanes(p, hw)], lambda i: ob.at[i]),
        "x": (3, lambda p: x.at[:, lanes(p, fw)], lambda i: xb.at[i]),
        "u": (4, lambda p: u2send.at[p], lambda i: u2.at[i]),
        "low": (5, lambda p: lowsend.at[p], lambda i: lowr.at[i]),
        "vg": (6, lambda p: vgsend.at[p], lambda i: vgr.at[i]),
        "bl": (7, lambda p: blr.at[s], lambda i: blr.at[i]),
        "ut": (8, lambda p: utsend.at[p], lambda i: utr.at[i]),
    }
    grp_kinds = {
        "a": (0, lambda p: asend.at[pl.ds(p * cap, cap)], lambda i: acand.at[pl.ds(i * cap, cap)]),
        "b": (1, lambda p: usend.at[pl.ds(p * cap, cap)], lambda i: ucand.at[pl.ds(i * cap, cap)]),
        "d": (2, lambda p: dsend.at[p], lambda i: down_out.at[i]),
        "t": (3, lambda p: tsend.at[p], lambda i: up_out.at[i]),
    }

    def send_one(name, peer):
        kind, src, dst = seq_kinds[name]
        seq_copy(kind, src(peer), dst(s), peer, s).start()

    def wait_one(name, origin):
        kind, src, dst = seq_kinds[name]
        seq_copy(kind, src(origin), dst(origin), origin, origin).wait_recv()

    def each_peer(fn, me, count):
        def body(step, carry):
            fn(lax.rem(me + step, count))
            return carry
        lax.fori_loop(1, count, body, 0)

    def send_seq(name):
        each_peer(lambda p: send_one(name, p), s, n)

    def wait_seq(name):
        each_peer(lambda p: wait_one(name, p), s, n)

    def sent_seq(name):
        kind, src, dst = seq_kinds[name]
        each_peer(lambda p: seq_copy(kind, src(p), dst(s), p, s).wait_send(), s, n)

    def send_grp_one(name, peer):
        kind, src, dst = grp_kinds[name]
        grp_copy(kind, src(peer), dst(g), peer, g).start()

    def wait_grp(name):
        kind, src, dst = grp_kinds[name]
        each_peer(lambda p: grp_copy(kind, src(p), dst(p), p, p).wait_recv(), g, groups)

    def sent_grp(name):
        kind, src, dst = grp_kinds[name]
        each_peer(lambda p: grp_copy(kind, src(p), dst(g), p, g).wait_send(), g, groups)

    barrier = pltpu.get_barrier_semaphore()

    def greet_seq(p):
        pl.semaphore_signal(barrier, inc=1, device_id={"seq": p}, device_id_type=MESH)

    def greet_grp(p):
        pl.semaphore_signal(barrier, inc=1, device_id={"grp": p}, device_id_type=MESH)

    each_peer(greet_seq, s, n)
    each_peer(greet_grp, g, groups)

    own = {}
    for number, name in enumerate(("k", "q", "o", "x")):
        _, src, dst = seq_kinds[name]
        own[name] = pltpu.make_async_copy(src(s), dst(s), near.at[number])
    own["a"] = pltpu.make_async_copy(ad, adv, near.at[4])
    own["b"] = pltpu.make_async_copy(au, auv, near.at[5])
    for name in ("a", "b", "k", "q", "o", "x"):
        own[name].start()

    chosen_rows(sai, row, g, sel_s, groups, segs, resident, cap, 0)
    owners, ranks, places, _ = segment_places(sai, row, g, segs, resident, cap)
    ends = []
    total = jnp.int32(0)
    for j in range(segs):
        total = total + cnt[g, j]
        ends.append(total)
    for b in range(pad):
        seg_s[b] = jnp.int32(-1)

    def one_block(b, carry):
        seg = jnp.int32(0)
        for j in range(segs):
            seg = seg + jnp.where(b >= ends[j], 1, 0)
        place = jnp.int32(0)
        for j in range(segs):
            place = jnp.where(seg == j, places[j], place)
        seg_s[pad + b] = seg
        place_s[b] = place
        return carry

    lax.fori_loop(0, n, one_block, 0)

    def partner(step):
        index, bit = 0, 1
        while bit < n:
            ours, flip = (s // bit) % 2, (step // bit) % 2
            index = index + (ours + flip - 2 * ours * flip) * bit
            bit *= 2
        return index

    def send_heads(p):
        for name in ("q", "o"):
            send_one(name, p)

    order = [1, 2, 4, 6, 3, 5, 7] if n == 8 else list(range(1, n))
    ahead = min(4, n - 1)
    pl.semaphore_wait(barrier, n - 1 + groups - 1)
    send_seq("k")
    for step in order[:ahead]:
        send_heads(partner(step))

    own["a"].wait()
    own["b"].wait()

    def pick(slot, carry):
        index = sel_s[slot]
        asend[slot] = adv[index]
        usend[slot] = auv[index]
        return carry

    lax.fori_loop(0, groups * cap, pick, 0)
    each_peer(lambda p: send_grp_one("b", p), g, groups)
    each_peer(lambda p: send_grp_one("a", p), g, groups)
    for c in range(cap):
        acand[g * cap + c] = asend[g * cap + c]
        ucand[g * cap + c] = usend[g * cap + c]
    for b in range(pad):
        kb[b] = jnp.zeros_like(kb[b])
    acc[...] = jnp.zeros_like(acc)

    def route(b, carry):
        u2send[b] = ucand[place_s[b]]
        return carry

    def route_up():
        wait_grp("b")
        lax.fori_loop(0, n, route, 0)
        send_seq("u")
        u2[s] = u2send[s]

    factor = math.log2(math.e) / math.sqrt(HEAD_DIM)

    def attend(b, first, count):
        width = count * blk
        queries = jnp.concatenate(
            [qb[b, :, h * HEAD_DIM:(h + 1) * HEAD_DIM] for h in range(hh)], 0)
        grads = jnp.concatenate(
            [ob[b, :, h * HEAD_DIM:(h + 1) * HEAD_DIM] for h in range(hh)], 0)
        keys = kb[pl.ds(first, count)].reshape(width, HEAD_DIM)
        scores = lax.dot_general(queries, keys, (((1,), (1,)), ((), ())),
                                 preferred_element_type=F32)
        column = lax.broadcasted_iota(jnp.int32, (1, width), 1)
        ids = jnp.full((1, width), seg_s[first], jnp.int32)
        for j in range(1, count):
            ids = jnp.where(column >= j * blk, seg_s[first + j], ids)
        rows = lax.broadcasted_iota(jnp.int32, (blk, width), 0)
        columns = lax.broadcasted_iota(jnp.int32, (blk, width), 1)
        seen = (ids == seg_s[pad + b]) & (columns - (count - 1) * blk <= rows)
        bias = jnp.where(seen, F32(0), F32(-1e30))
        scores = (scores.reshape(hh, blk, width) + bias[None]).reshape(hh * blk, width)
        highest = jnp.max(scores, axis=1, keepdims=True)
        expo = jnp.exp2((scores - highest) * factor)
        probs = (expo * (1.0 / jnp.sum(expo, axis=1, keepdims=True))).astype(BF16)
        part = lax.dot_general(probs, grads, (((0,), (0,)), ((), ())),
                               preferred_element_type=F32)
        acc[pl.ds(first, count)] += part.reshape(count, blk, HEAD_DIM)

    own["k"].wait()
    own["q"].wait()
    own["o"].wait()
    wait_seq("k")
    attend(s, s, reach)

    def visit(b):
        wait_one("q", b)
        wait_one("o", b)
        attend(b, b, reach)

    early = 0
    if n == 8:
        for number, step in enumerate(order):
            if number >= 1 and number - 1 + ahead < n - 1:
                send_heads(partner(order[number - 1 + ahead]))
            if number == 2:
                route_up()
            if number == 4:
                early = 4
                for other in order[:early]:
                    send_one("x", partner(other))
            visit(partner(step))
    else:
        route_up()

        def one_step(step, carry):
            @pl.when(step + ahead < n)
            def _():
                send_heads(partner(step + ahead))

            visit(partner(step))
            return carry

        lax.fori_loop(1, n, one_step, 0)

    def finish(step, carry):
        b = partner(step)
        vgsend[b] = acc[pad + b].astype(BF16)
        send_one("vg", b)
        return carry

    lax.fori_loop(1, n, finish, 0)
    vgr[s] = acc[pad + s].astype(BF16)
    for step in order[early:]:
        send_one("x", partner(step))

    wait_seq("u")
    for i in range(n):
        uf[i * rp:(i + 1) * rp, :] = u2[i].astype(F32)
    up_rows = uf[...].astype(BF16)
    wait_seq("vg")
    share = gs // hh
    heads = []
    for kv in range(n // share):
        if share == 1:
            heads.append(vgr[kv])
        else:
            whole = vgr[kv * share].astype(F32)
            for i in range(1, share):
                whole = whole + vgr[kv * share + i].astype(F32)
            heads.append(whole.astype(BF16))
    value_grad = jnp.concatenate(heads, 1)
    back = SCALE * lax.dot_general(up_rows, value_grad, (((1,), (1,)), ((), ())),
                                   preferred_element_type=F32)
    blr[s] = back.astype(BF16)
    send_seq("bl")

    wait_grp("a")
    own["x"].wait()
    wait_seq("x")

    def lowered(b, carry):
        lowsend[b] = lax.dot_general(acand[place_s[b]], xb[b], (((1,), (1,)), ((), ())),
                                     preferred_element_type=F32)
        return carry

    lax.fori_loop(0, n, lowered, 0)
    send_seq("low")
    lowr[s] = lowsend[s]

    wait_seq("bl")
    features = xb[...].reshape(n * blk, fw)

    def down_terms(peer):
        rows = []
        for c in range(cap):
            rows.append(jnp.concatenate(
                [jnp.where(place_s[b] == peer * cap + c, blr[b].astype(F32), F32(0)).astype(BF16)
                 for b in range(n)], 1))
        dsend[peer] = lax.dot_general(jnp.concatenate(rows, 0), features,
                                      (((1,), (0,)), ((), ())),
                                      preferred_element_type=F32).astype(BF16)

    def down_send(peer):
        down_terms(peer)
        send_grp_one("d", peer)

    each_peer(down_send, g, groups)
    down_terms(g)
    mine_down = pltpu.make_async_copy(dsend.at[g], down_out.at[g], near.at[6])
    mine_down.start()

    wait_seq("low")
    low = lowr[0]
    for i in range(1, n):
        low = low + lowr[i]
    terms = SCALE * lax.dot_general(low.astype(BF16), value_grad, (((1,), (0,)), ((), ())),
                                    preferred_element_type=F32)
    for i in range(n):
        utsend[i] = terms[i * rp:(i + 1) * rp, :]
    send_seq("ut")
    utr[s] = utsend[s]
    wait_seq("ut")

    def up_terms(peer):
        for c in range(cap):
            def add(b, total):
                return total + jnp.where(place_s[b] == peer * cap + c, utr[b], F32(0))
            tf[c * rp:(c + 1) * rp, :] = lax.fori_loop(
                0, n, add, jnp.zeros(utr.shape[1:], F32))
        tsend[peer] = tf[...].astype(BF16)

    def up_send(peer):
        up_terms(peer)
        send_grp_one("t", peer)

    each_peer(up_send, g, groups)
    up_terms(g)
    mine_up = pltpu.make_async_copy(tsend.at[g], up_out.at[g], near.at[7])
    mine_up.start()

    for name in seq_kinds:
        sent_seq(name)
    for name in grp_kinds:
        sent_grp(name)
    mine_down.wait()
    mine_up.wait()
    wait_grp("d")
    wait_grp("t")


def spread_kernel(cfg, sai, row, down, up, down_grad, up_grad, sel_s):
    groups, cap, segs, resident, rank, rp = cfg
    step = pl.program_id(0)
    here = down_grad.shape[0]
    g = lax.axis_index("grp")

    @pl.when(step == 0)
    def _():
        chosen_rows(sai, row, g, sel_s, groups, segs, resident, cap, -1)

    def rows_of(terms, ranks):
        count = groups * cap
        slots = lax.broadcasted_iota(jnp.int32, (1, count * ranks), 1)
        target = jnp.full((1, count * ranks), -1, jnp.int32)
        for i in range(count):
            inside = (slots >= i * ranks) & (slots < (i + 1) * ranks)
            first = jnp.where(sel_s[i] < 0, -(1 << 20), (sel_s[i] - step * here) * ranks)
            target = jnp.where(inside, first + slots - i * ranks, target)
        rows = lax.broadcasted_iota(jnp.int32, (here * ranks, count * ranks), 0)
        onehot = jnp.where(rows == target, F32(1), F32(0)).astype(BF16)
        return lax.dot_general(onehot, terms, (((1,), (0,)), ((), ())), preferred_element_type=F32)

    down_grad[...] = rows_of(down[...], rank).reshape(down_grad.shape)
    up_grad[...] = rows_of(up[...], rp).reshape(up_grad.shape)


def local(x, q, k, o, ad, au, sai, cnt, row):
    groups = lax.axis_size("grp")
    n = lax.axis_size("seq")
    tokens = x.shape[0]
    fw = ad.shape[2]
    resident, rank = ad.shape[0], ad.shape[1]
    rp, vw = au.shape[1], au.shape[2]
    segs = sai.shape[1]
    cap = max(2, (segs + groups - 1) // groups)
    reach = min(16, n * tokens // (2 * BLOCK))
    heads = q.shape[1] // HEAD_DIM
    hh = heads // n
    gs = heads // (vw // HEAD_DIM)
    assert tokens == BLOCK and gs % hh == 0 and n & (n - 1) == 0
    pad = reach - 1
    cfg = (n, groups, cap, segs, resident, rank, rp, fw, hh, gs, reach, pad)
    slots = groups * cap
    smem = pl.BlockSpec(memory_space=pltpu.SMEM)
    hbm = pl.BlockSpec(memory_space=pl.ANY)
    down, up = pl.pallas_call(
        functools.partial(exchange_kernel, cfg),
        out_shape=(
            jax.ShapeDtypeStruct((groups, cap * rank, fw), BF16),
            jax.ShapeDtypeStruct((groups, cap * rp, vw), BF16),
        ),
        in_specs=[smem] * 3 + [pl.BlockSpec(memory_space=pltpu.HBM)] * 6,
        out_specs=(hbm, hbm),
        scratch_shapes=[
            pltpu.SMEM((n + pad,), jnp.int32),
            pltpu.SMEM((n,), jnp.int32),
            pltpu.SMEM((slots,), jnp.int32),
            pltpu.VMEM((n, BLOCK, hh * HEAD_DIM), BF16),
            pltpu.VMEM((n, BLOCK, hh * HEAD_DIM), BF16),
            pltpu.VMEM((n + pad, BLOCK, HEAD_DIM), BF16),
            pltpu.VMEM((n, BLOCK, fw), BF16),
            pltpu.VMEM(ad.shape, BF16),
            pltpu.VMEM(au.shape, BF16),
            pltpu.VMEM((slots, rank, fw), BF16),
            pltpu.VMEM((slots, rp, vw), BF16),
            pltpu.VMEM((slots, rank, fw), BF16),
            pltpu.VMEM((slots, rp, vw), BF16),
            pltpu.VMEM((n, rp, vw), BF16),
            pltpu.VMEM((n, rp, vw), BF16),
            pltpu.VMEM((rank, vw), F32),
            pltpu.VMEM((n, rank, BLOCK), F32),
            pltpu.VMEM((n, rank, BLOCK), F32),
            pltpu.VMEM((n, BLOCK, HEAD_DIM), BF16),
            pltpu.VMEM((n, BLOCK, HEAD_DIM), BF16),
            pltpu.VMEM((n, rank, BLOCK), BF16),
            pltpu.VMEM((n, rp, vw), F32),
            pltpu.VMEM((n, rp, vw), F32),
            pltpu.VMEM((groups, cap * rank, fw), BF16),
            pltpu.VMEM((cap * rp, vw), F32),
            pltpu.VMEM((groups, cap * rp, vw), BF16),
            pltpu.VMEM((n + pad, BLOCK, HEAD_DIM), F32),
            pltpu.SemaphoreType.DMA((9, n)),
            pltpu.SemaphoreType.DMA((9, n)),
            pltpu.SemaphoreType.DMA((4, groups)),
            pltpu.SemaphoreType.DMA((4, groups)),
            pltpu.SemaphoreType.DMA((8,)),
        ],
        compiler_params=pltpu.CompilerParams(
            collective_id=0, has_side_effects=True, vmem_limit_bytes=60 * 1024 * 1024),
        name="exchange",
    )(sai, cnt, row, x, q, k, o, ad, au)
    steps = 4
    here = resident // steps
    return pl.pallas_call(
        functools.partial(spread_kernel, (groups, cap, segs, resident, rank, rp)),
        grid=(steps,),
        out_shape=(
            jax.ShapeDtypeStruct((resident, rank, fw), F32),
            jax.ShapeDtypeStruct((resident, rp, vw), F32),
        ),
        in_specs=[
            smem, smem,
            pl.BlockSpec((slots * rank, fw), lambda i: (0, 0)),
            pl.BlockSpec((slots * rp, vw), lambda i: (0, 0)),
        ],
        out_specs=(
            pl.BlockSpec((here, rank, fw), lambda i: (i, 0, 0)),
            pl.BlockSpec((here, rp, vw), lambda i: (i, 0, 0)),
        ),
        scratch_shapes=[pltpu.SMEM((slots,), jnp.int32)],
        compiler_params=pltpu.CompilerParams(vmem_limit_bytes=60 * 1024 * 1024),
        name="spread",
    )(sai, row, down.reshape(slots * rank, fw), up.reshape(slots * rp, vw))


def solution(mesh):
    return jax.shard_map(
        local,
        mesh=mesh,
        in_specs=(
            P(("grp", "seq"), None),
            P(("grp", "seq"), None),
            P(("grp", "seq"), None),
            P(("grp", "seq"), None),
            P("grp", None, "seq"),
            P("grp", "seq", None),
            P(),
            P(),
            P(),
        ),
        out_specs=(P("grp", None, "seq"), P("grp", "seq", None)),
        check_vma=False,
    )
```

```python
import functools
import math

import jax
import jax.numpy as jnp
from jax import lax
from jax.experimental import pallas as pl
from jax.experimental.pallas import tpu as pltpu
from jax.sharding import PartitionSpec as P

HEAD_DIM = 128
BLOCK = 128
SCALE = 2.0
MESH = pl.DeviceIdType.MESH
F32 = jnp.float32
BF16 = jnp.bfloat16


def segment_places(sai, row, seq, segs, resident, cap):
    owners, places, locals_ = [], [], []
    ranks = []
    for j in range(segs):
        slot = row[sai[seq, j]]
        owner = slot // resident
        rank = jnp.int32(0)
        for i in range(j):
            rank = rank + jnp.where(owners[i] == owner, 1, 0)
        owners.append(owner)
        ranks.append(rank)
        places.append(owner * cap + rank)
        locals_.append(slot - owner * resident)
    return owners, ranks, places, locals_


def chosen_rows(sai, row, group, sel, groups, segs, resident, cap):
    def one(seq, carry):
        owners, ranks, _, held = segment_places(sai, row, seq, segs, resident, cap)
        for c in range(cap):
            value = jnp.int32(-1)
            for j in range(segs):
                value = jnp.where((owners[j] == group) & (ranks[j] == c), held[j], value)
            sel[seq * cap + c] = value
        return carry

    lax.fori_loop(0, groups, one, 0)


def exchange_kernel(
    cfg, sai, cnt, row, x, q, k, o, ad, au, down_out, up_out, sel_s,
    seg_s, place_s,
    qb, ob, kb, xb, adv, auv, asend, usend, acand, ucand, u2send, u2, uf,
    lowsend, lowr, vgsend, vgr, blr, utsend, utr, masked, dsend, tf, tsend, acc,
    seq_send, seq_recv, grp_send, grp_recv, near,
):
    n, groups, cap, segs, resident, rank, rp, fw, hh, gs, reach, pad, chunks = cfg
    fc = fw // chunks
    s = lax.axis_index("seq")
    g = lax.axis_index("grp")
    hw = hh * HEAD_DIM
    blk = BLOCK

    def lanes(index, width):
        return pl.ds(pl.multiple_of(index * width, 128), width)

    def seq_copy(kind, src, dst, peer, origin):
        return pltpu.make_async_remote_copy(
            src_ref=src, dst_ref=dst, send_sem=seq_send.at[kind, peer],
            recv_sem=seq_recv.at[kind, origin], device_id={"seq": peer}, device_id_type=MESH)

    def grp_copy(kind, src, dst, peer, origin):
        return pltpu.make_async_remote_copy(
            src_ref=src, dst_ref=dst, send_sem=grp_send.at[kind, peer],
            recv_sem=grp_recv.at[kind, origin], device_id={"grp": peer}, device_id_type=MESH)

    def key_src(p):
        return k.at[:, lanes((p * hh) // gs, HEAD_DIM)]

    seq_kinds = {
        "k": (0, key_src, lambda i: kb.at[pad + i]),
        "q": (1, lambda p: q.at[:, lanes(p, hw)], lambda i: qb.at[i]),
        "o": (2, lambda p: o.at[:, lanes(p, hw)], lambda i: ob.at[i]),
        "u": (4, lambda p: u2send.at[p], lambda i: u2.at[i]),
        "low": (5, lambda p: lowsend.at[p], lambda i: lowr.at[i]),
        "vg": (6, lambda p: vgsend.at[p], lambda i: vgr.at[i]),
        "bl": (7, lambda p: blr.at[s], lambda i: blr.at[i]),
        "ut": (8, lambda p: utsend.at[p], lambda i: utr.at[i]),
    }
    for part in range(chunks):
        seq_kinds["x", part] = (
            3 if part == 0 else 8 + part,
            lambda p, part=part: x.at[:, lanes(p * chunks + part, fc)],
            lambda i, part=part: xb.at[part, i])
    grp_kinds = {
        "a": (0, lambda p: asend.at[pl.ds(p * cap, cap)], lambda i: acand.at[pl.ds(i * cap, cap)]),
        "b": (1, lambda p: usend.at[pl.ds(p * cap, cap)], lambda i: ucand.at[pl.ds(i * cap, cap)]),
        "t": (2, lambda p: tsend.at[p], lambda i: up_out.at[i]),
    }
    for part in range(chunks):
        grp_kinds["d", part] = (
            3 + part,
            lambda p, part=part: dsend.at[part, p],
            lambda i, part=part: down_out.at[i, :, part * fc:(part + 1) * fc])

    def send_one(name, peer):
        kind, src, dst = seq_kinds[name]
        seq_copy(kind, src(peer), dst(s), peer, s).start()

    def wait_one(name, origin):
        kind, src, dst = seq_kinds[name]
        seq_copy(kind, src(origin), dst(origin), origin, origin).wait_recv()

    def each_peer(fn, me, count):
        def body(step, carry):
            fn(lax.rem(me + step, count))
            return carry
        lax.fori_loop(1, count, body, 0)

    def send_seq(name):
        each_peer(lambda p: send_one(name, p), s, n)

    def wait_seq(name):
        each_peer(lambda p: wait_one(name, p), s, n)

    def sent_seq(name):
        kind, src, dst = seq_kinds[name]
        each_peer(lambda p: seq_copy(kind, src(p), dst(s), p, s).wait_send(), s, n)

    def send_grp_one(name, peer):
        kind, src, dst = grp_kinds[name]
        grp_copy(kind, src(peer), dst(g), peer, g).start()

    def wait_grp(name):
        kind, src, dst = grp_kinds[name]
        each_peer(lambda p: grp_copy(kind, src(p), dst(p), p, p).wait_recv(), g, groups)

    def sent_grp(name):
        kind, src, dst = grp_kinds[name]
        each_peer(lambda p: grp_copy(kind, src(p), dst(g), p, g).wait_send(), g, groups)

    barrier = pltpu.get_barrier_semaphore()

    def greet_seq(p):
        pl.semaphore_signal(barrier, inc=1, device_id={"seq": p}, device_id_type=MESH)

    def greet_grp(p):
        pl.semaphore_signal(barrier, inc=1, device_id={"grp": p}, device_id_type=MESH)

    each_peer(greet_seq, s, n)
    each_peer(greet_grp, g, groups)

    own = {}
    x_parts = [("x", part) for part in range(chunks)]
    for number, name in enumerate(["k", "q", "o"] + x_parts):
        _, src, dst = seq_kinds[name]
        own[name] = pltpu.make_async_copy(src(s), dst(s), near.at[number])
    own["a"] = pltpu.make_async_copy(ad, adv, near.at[3 + chunks])
    own["b"] = pltpu.make_async_copy(au, auv, near.at[4 + chunks])
    for name in ["a", "b", "k", "q", "o"] + x_parts:
        own[name].start()

    chosen_rows(sai, row, g, sel_s, groups, segs, resident, cap)
    owners, ranks, places, _ = segment_places(sai, row, g, segs, resident, cap)
    ends = []
    total = jnp.int32(0)
    for j in range(segs):
        total = total + cnt[g, j]
        ends.append(total)
    for b in range(pad):
        seg_s[b] = jnp.int32(-1)

    def one_block(b, carry):
        seg = jnp.int32(0)
        for j in range(segs):
            seg = seg + jnp.where(b >= ends[j], 1, 0)
        place = jnp.int32(0)
        for j in range(segs):
            place = jnp.where(seg == j, places[j], place)
        seg_s[pad + b] = seg
        place_s[b] = place
        return carry

    lax.fori_loop(0, n, one_block, 0)

    def partner(step):
        index, bit = 0, 1
        while bit < n:
            ours, flip = (s // bit) % 2, (step // bit) % 2
            index = index + (ours + flip - 2 * ours * flip) * bit
            bit *= 2
        return index

    def send_heads(p):
        for name in ("q", "o"):
            send_one(name, p)

    order = [1, 2, 4, 6, 3, 5, 7] if n == 8 else list(range(1, n))
    ahead = min(4, n - 1)
    pl.semaphore_wait(barrier, n - 1 + groups - 1)
    send_seq("k")
    for step in order[:ahead]:
        send_heads(partner(step))

    own["a"].wait()
    own["b"].wait()

    def pick(slot, carry):
        index = jnp.maximum(sel_s[slot], 0)
        asend[slot] = adv[index]
        usend[slot] = auv[index]
        return carry

    lax.fori_loop(0, groups * cap, pick, 0)
    each_peer(lambda p: send_grp_one("b", p), g, groups)
    each_peer(lambda p: send_grp_one("a", p), g, groups)
    for c in range(cap):
        acand[g * cap + c] = asend[g * cap + c]
        ucand[g * cap + c] = usend[g * cap + c]
    for b in range(pad):
        kb[b] = jnp.zeros_like(kb[b])
    acc[...] = jnp.zeros_like(acc)

    def route(b, carry):
        u2send[b] = ucand[place_s[b]]
        return carry

    def route_up():
        wait_grp("b")
        lax.fori_loop(0, n, route, 0)
        send_seq("u")
        u2[s] = u2send[s]

    factor = math.log2(math.e) / math.sqrt(HEAD_DIM)

    def attend(b, first, count):
        width = count * blk
        queries = jnp.concatenate(
            [qb[b, :, h * HEAD_DIM:(h + 1) * HEAD_DIM] for h in range(hh)], 0)
        grads = jnp.concatenate(
            [ob[b, :, h * HEAD_DIM:(h + 1) * HEAD_DIM] for h in range(hh)], 0)
        keys = kb[pl.ds(first, count)].reshape(width, HEAD_DIM)
        scores = lax.dot_general(queries, keys, (((1,), (1,)), ((), ())),
                                 preferred_element_type=F32)
        column = lax.broadcasted_iota(jnp.int32, (1, width), 1)
        ids = jnp.full((1, width), seg_s[first], jnp.int32)
        for j in range(1, count):
            ids = jnp.where(column >= j * blk, seg_s[first + j], ids)
        rows = lax.broadcasted_iota(jnp.int32, (blk, width), 0)
        columns = lax.broadcasted_iota(jnp.int32, (blk, width), 1)
        seen = (ids == seg_s[pad + b]) & (columns - (count - 1) * blk <= rows)
        bias = jnp.where(seen, F32(0), F32(-1e30))
        scores = (scores.reshape(hh, blk, width) + bias[None]).reshape(hh * blk, width)
        highest = jnp.max(scores, axis=1, keepdims=True)
        expo = jnp.exp2((scores - highest) * factor)
        probs = (expo * (1.0 / jnp.sum(expo, axis=1, keepdims=True))).astype(BF16)
        part = lax.dot_general(probs, grads, (((0,), (0,)), ((), ())),
                               preferred_element_type=F32)
        acc[pl.ds(first, count)] += part.reshape(count, blk, HEAD_DIM)

    own["k"].wait()
    own["q"].wait()
    own["o"].wait()
    wait_seq("k")
    attend(s, s, reach)

    def visit(b):
        wait_one("q", b)
        wait_one("o", b)
        attend(b, b, reach)

    first_x = n == 8
    if n == 8:
        for number, step in enumerate(order):
            if number >= 1 and number - 1 + ahead < n - 1:
                send_heads(partner(order[number - 1 + ahead]))
            if number == 2:
                route_up()
            if number == 4:
                for other in order:
                    send_one(x_parts[0], partner(other))
            visit(partner(step))
    else:
        route_up()

        def one_step(step, carry):
            @pl.when(step + ahead < n)
            def _():
                send_heads(partner(step + ahead))

            visit(partner(step))
            return carry

        lax.fori_loop(1, n, one_step, 0)

    def finish(step, carry):
        b = partner(step)
        vgsend[b] = acc[pad + b].astype(BF16)
        send_one("vg", b)
        return carry

    lax.fori_loop(1, n, finish, 0)
    vgr[s] = acc[pad + s].astype(BF16)
    if not first_x:
        send_seq(x_parts[0])
    half = (n - 1) // 2
    for name in x_parts[1:]:
        for step in order[:half]:
            send_one(name, partner(step))

    wait_seq("u")
    for i in range(n):
        uf[i * rp:(i + 1) * rp, :] = u2[i].astype(F32)
    up_rows = uf[...].astype(BF16)
    wait_seq("vg")
    share = gs // hh
    heads = []
    for kv in range(n // share):
        if share == 1:
            heads.append(vgr[kv])
        else:
            whole = vgr[kv * share].astype(F32)
            for i in range(1, share):
                whole = whole + vgr[kv * share + i].astype(F32)
            heads.append(whole.astype(BF16))
    value_grad = jnp.concatenate(heads, 1)
    back = SCALE * lax.dot_general(up_rows, value_grad, (((1,), (1,)), ((), ())),
                                   preferred_element_type=F32)
    blr[s] = back.astype(BF16)
    send_seq("bl")

    for name in x_parts[1:]:
        for step in order[half:]:
            send_one(name, partner(step))

    wait_seq("bl")
    for c in range(cap):
        for b in range(n):
            for owner in range(groups):
                masked[owner, c * rank:(c + 1) * rank, b * blk:(b + 1) * blk] = jnp.where(
                    place_s[b] == owner * cap + c, blr[b].astype(F32), F32(0)).astype(BF16)
    mine_down = []
    for part in range(chunks):
        own["x", part].wait()
        wait_seq(("x", part))
        features = xb[part].reshape(n * blk, fc)

        def down_terms(peer):
            dsend[part, peer] = lax.dot_general(
                masked[peer], features, (((1,), (0,)), ((), ())),
                preferred_element_type=F32).astype(BF16)

        def down_send(peer):
            down_terms(peer)
            send_grp_one(("d", part), peer)

        each_peer(down_send, g, groups)
        down_terms(g)
        _, src, dst = grp_kinds["d", part]
        mine_down.append(pltpu.make_async_copy(src(g), dst(g), near.at[6 + chunks + part]))
        mine_down[-1].start()

    wait_grp("a")

    def lowered(b, carry):
        weights = acand[place_s[b]]
        total = jnp.zeros((rank, blk), F32)
        for part in range(chunks):
            total = total + lax.dot_general(
                weights[:, part * fc:(part + 1) * fc], xb[part, b], (((1,), (1,)), ((), ())),
                preferred_element_type=F32)
        lowsend[b] = total.astype(BF16)
        return carry

    lax.fori_loop(0, n, lowered, 0)
    send_seq("low")
    lowr[s] = lowsend[s]

    wait_seq("low")
    low = lowr[0].astype(F32)
    for i in range(1, n):
        low = low + lowr[i].astype(F32)
    terms = SCALE * lax.dot_general(low.astype(BF16), value_grad, (((1,), (0,)), ((), ())),
                                    preferred_element_type=F32)
    for i in range(n):
        utsend[i] = terms[i * rp:(i + 1) * rp, :].astype(BF16)
    send_seq("ut")
    utr[s] = utsend[s]
    wait_seq("ut")

    def up_terms(peer):
        for c in range(cap):
            def add(b, total):
                return total + jnp.where(place_s[b] == peer * cap + c, utr[b].astype(F32), F32(0))
            tf[c * rp:(c + 1) * rp, :] = lax.fori_loop(
                0, n, add, jnp.zeros(utr.shape[1:], F32))
        tsend[peer] = tf[...].astype(BF16)

    def up_send(peer):
        up_terms(peer)
        send_grp_one("t", peer)

    each_peer(up_send, g, groups)
    up_terms(g)
    mine_up = pltpu.make_async_copy(tsend.at[g], up_out.at[g], near.at[5 + chunks])
    mine_up.start()

    for name in seq_kinds:
        sent_seq(name)
    for name in grp_kinds:
        sent_grp(name)
    for copy in mine_down:
        copy.wait()
    mine_up.wait()
    for part in range(chunks):
        wait_grp(("d", part))
    wait_grp("t")


def spread_kernel(cfg, sel_s, down, up, down_grad, up_grad):
    groups, cap, rank, rp = cfg
    step = pl.program_id(0)
    here = down_grad.shape[0]
    def rows_of(terms, ranks):
        count = groups * cap
        slots = lax.broadcasted_iota(jnp.int32, (1, count * ranks), 1)
        target = jnp.full((1, count * ranks), -1, jnp.int32)
        for i in range(count):
            inside = (slots >= i * ranks) & (slots < (i + 1) * ranks)
            first = jnp.where(sel_s[i] < 0, -(1 << 20), (sel_s[i] - step * here) * ranks)
            target = jnp.where(inside, first + slots - i * ranks, target)
        rows = lax.broadcasted_iota(jnp.int32, (here * ranks, count * ranks), 0)
        onehot = jnp.where(rows == target, F32(1), F32(0)).astype(BF16)
        return lax.dot_general(onehot, terms, (((1,), (0,)), ((), ())), preferred_element_type=F32)

    down_grad[...] = rows_of(down[...], rank).reshape(down_grad.shape)
    up_grad[...] = rows_of(up[...], rp).reshape(up_grad.shape)


def local(x, q, k, o, ad, au, sai, cnt, row):
    groups = lax.axis_size("grp")
    n = lax.axis_size("seq")
    tokens = x.shape[0]
    fw = ad.shape[2]
    resident, rank = ad.shape[0], ad.shape[1]
    rp, vw = au.shape[1], au.shape[2]
    segs = sai.shape[1]
    cap = max(2, (segs + groups - 1) // groups)
    reach = min(16, n * tokens // (2 * BLOCK))
    heads = q.shape[1] // HEAD_DIM
    hh = heads // n
    gs = heads // (vw // HEAD_DIM)
    assert tokens == BLOCK and gs % hh == 0 and n & (n - 1) == 0
    pad = reach - 1
    chunks = 2 if fw % 256 == 0 else 1
    cfg = (n, groups, cap, segs, resident, rank, rp, fw, hh, gs, reach, pad, chunks)
    slots = groups * cap
    smem = pl.BlockSpec(memory_space=pltpu.SMEM)
    hbm = pl.BlockSpec(memory_space=pl.ANY)
    down, up, sel = pl.pallas_call(
        functools.partial(exchange_kernel, cfg),
        out_shape=(
            jax.ShapeDtypeStruct((groups, cap * rank, fw), BF16),
            jax.ShapeDtypeStruct((groups, cap * rp, vw), BF16),
            jax.ShapeDtypeStruct((slots,), jnp.int32),
        ),
        in_specs=[smem] * 3 + [pl.BlockSpec(memory_space=pltpu.HBM)] * 6,
        out_specs=(hbm, hbm, smem),
        scratch_shapes=[
            pltpu.SMEM((n + pad,), jnp.int32),
            pltpu.SMEM((n,), jnp.int32),
            pltpu.VMEM((n, BLOCK, hh * HEAD_DIM), BF16),
            pltpu.VMEM((n, BLOCK, hh * HEAD_DIM), BF16),
            pltpu.VMEM((n + pad, BLOCK, HEAD_DIM), BF16),
            pltpu.VMEM((chunks, n, BLOCK, fw // chunks), BF16),
            pltpu.VMEM(ad.shape, BF16),
            pltpu.VMEM(au.shape, BF16),
            pltpu.VMEM((slots, rank, fw), BF16),
            pltpu.VMEM((slots, rp, vw), BF16),
            pltpu.VMEM((slots, rank, fw), BF16),
            pltpu.VMEM((slots, rp, vw), BF16),
            pltpu.VMEM((n, rp, vw), BF16),
            pltpu.VMEM((n, rp, vw), BF16),
            pltpu.VMEM((rank, vw), F32),
            pltpu.VMEM((n, rank, BLOCK), BF16),
            pltpu.VMEM((n, rank, BLOCK), BF16),
            pltpu.VMEM((n, BLOCK, HEAD_DIM), BF16),
            pltpu.VMEM((n, BLOCK, HEAD_DIM), BF16),
            pltpu.VMEM((n, rank, BLOCK), BF16),
            pltpu.VMEM((n, rp, vw), BF16),
            pltpu.VMEM((n, rp, vw), BF16),
            pltpu.VMEM((groups, cap * rank, n * BLOCK), BF16),
            pltpu.VMEM((chunks, groups, cap * rank, fw // chunks), BF16),
            pltpu.VMEM((cap * rp, vw), F32),
            pltpu.VMEM((groups, cap * rp, vw), BF16),
            pltpu.VMEM((n + pad, BLOCK, HEAD_DIM), F32),
            pltpu.SemaphoreType.DMA((8 + chunks, n)),
            pltpu.SemaphoreType.DMA((8 + chunks, n)),
            pltpu.SemaphoreType.DMA((3 + chunks, groups)),
            pltpu.SemaphoreType.DMA((3 + chunks, groups)),
            pltpu.SemaphoreType.DMA((6 + 2 * chunks,)),
        ],
        compiler_params=pltpu.CompilerParams(
            collective_id=0, has_side_effects=True, vmem_limit_bytes=60 * 1024 * 1024),
        name="exchange",
    )(sai, cnt, row, x, q, k, o, ad, au)
    steps = 4
    here = resident // steps
    return pl.pallas_call(
        functools.partial(spread_kernel, (groups, cap, rank, rp)),
        grid=(steps,),
        out_shape=(
            jax.ShapeDtypeStruct((resident, rank, fw), F32),
            jax.ShapeDtypeStruct((resident, rp, vw), F32),
        ),
        in_specs=[
            smem,
            pl.BlockSpec((slots * rank, fw), lambda i: (0, 0)),
            pl.BlockSpec((slots * rp, vw), lambda i: (0, 0)),
        ],
        out_specs=(
            pl.BlockSpec((here, rank, fw), lambda i: (i, 0, 0)),
            pl.BlockSpec((here, rp, vw), lambda i: (i, 0, 0)),
        ),
        compiler_params=pltpu.CompilerParams(vmem_limit_bytes=60 * 1024 * 1024),
        name="spread",
    )(sel, down.reshape(slots * rank, fw), up.reshape(slots * rp, vw))


def solution(mesh):
    return jax.shard_map(
        local,
        mesh=mesh,
        in_specs=(
            P(("grp", "seq"), None),
            P(("grp", "seq"), None),
            P(("grp", "seq"), None),
            P(("grp", "seq"), None),
            P("grp", None, "seq"),
            P("grp", "seq", None),
            P(),
            P(),
            P(),
        ),
        out_specs=(P("grp", None, "seq"), P("grp", "seq", None)),
        check_vma=False,
    )
```

```python
import functools
import math

import jax
import jax.numpy as jnp
from jax import lax
from jax.experimental import pallas as pl
from jax.experimental.pallas import tpu as pltpu
from jax.sharding import PartitionSpec as P

HEAD_DIM = 128
BLOCK = 128
SCALE = 2.0
MESH = pl.DeviceIdType.MESH
F32 = jnp.float32
BF16 = jnp.bfloat16


def segment_places(sai, row, seq, segs, resident, cap):
    owners, places, locals_ = [], [], []
    ranks = []
    for j in range(segs):
        slot = row[sai[seq, j]]
        owner = slot // resident
        rank = jnp.int32(0)
        for i in range(j):
            rank = rank + jnp.where(owners[i] == owner, 1, 0)
        owners.append(owner)
        ranks.append(rank)
        places.append(owner * cap + rank)
        locals_.append(slot - owner * resident)
    return owners, ranks, places, locals_


def chosen_rows(sai, row, group, sel, groups, segs, resident, cap):
    def one(seq, carry):
        owners, ranks, _, held = segment_places(sai, row, seq, segs, resident, cap)
        for c in range(cap):
            value = jnp.int32(-1)
            for j in range(segs):
                value = jnp.where((owners[j] == group) & (ranks[j] == c), held[j], value)
            sel[seq * cap + c] = value
        return carry

    lax.fori_loop(0, groups, one, 0)


def exchange_kernel(
    cfg, sai, cnt, row, x, q, k, o, ad, au, down_out, up_out, sel_s,
    seg_s, place_s,
    qb, ob, kb, xb, adv, auv, asend, usend, acand, ucand, u2send, u2, uf,
    lowsend, lowr, vgsend, vgr, blr, utsend, utr, masked, dsend, tf, tsend, acc,
    seq_send, seq_recv, grp_send, grp_recv, near,
):
    n, groups, cap, segs, resident, rank, rp, fw, hh, gs, reach, pad, chunks = cfg
    fc = fw // chunks
    s = lax.axis_index("seq")
    g = lax.axis_index("grp")
    hw = hh * HEAD_DIM
    blk = BLOCK

    def lanes(index, width):
        return pl.ds(pl.multiple_of(index * width, 128), width)

    def seq_copy(kind, src, dst, peer, origin):
        return pltpu.make_async_remote_copy(
            src_ref=src, dst_ref=dst, send_sem=seq_send.at[kind, peer],
            recv_sem=seq_recv.at[kind, origin], device_id={"seq": peer}, device_id_type=MESH)

    def grp_copy(kind, src, dst, peer, origin):
        return pltpu.make_async_remote_copy(
            src_ref=src, dst_ref=dst, send_sem=grp_send.at[kind, peer],
            recv_sem=grp_recv.at[kind, origin], device_id={"grp": peer}, device_id_type=MESH)

    def key_src(p):
        return k.at[:, lanes((p * hh) // gs, HEAD_DIM)]

    seq_kinds = {
        "k": (0, key_src, lambda i: kb.at[pad + i]),
        "q": (1, lambda p: q.at[:, lanes(p, hw)], lambda i: qb.at[i]),
        "o": (2, lambda p: o.at[:, lanes(p, hw)], lambda i: ob.at[i]),
        "u": (4, lambda p: u2send.at[p], lambda i: u2.at[i]),
        "low": (5, lambda p: lowsend.at[p], lambda i: lowr.at[i]),
        "vg": (6, lambda p: vgsend.at[p], lambda i: vgr.at[i]),
        "bl": (7, lambda p: blr.at[s], lambda i: blr.at[i]),
        "ut": (8, lambda p: utsend.at[p], lambda i: utr.at[i]),
    }
    for part in range(chunks):
        seq_kinds["x", part] = (
            3 if part == 0 else 8 + part,
            lambda p, part=part: x.at[:, lanes(p * chunks + part, fc)],
            lambda i, part=part: xb.at[part, i])
    grp_kinds = {
        "a": (0, lambda p: asend.at[pl.ds(p * cap, cap)], lambda i: acand.at[pl.ds(i * cap, cap)]),
        "b": (1, lambda p: usend.at[pl.ds(p * cap, cap)], lambda i: ucand.at[pl.ds(i * cap, cap)]),
        "t": (2, lambda p: tsend.at[p], lambda i: up_out.at[i]),
    }
    for part in range(chunks):
        grp_kinds["d", part] = (
            3 + part,
            lambda p, part=part: dsend.at[part, p],
            lambda i, part=part: down_out.at[i, :, part * fc:(part + 1) * fc])

    def send_one(name, peer):
        kind, src, dst = seq_kinds[name]
        seq_copy(kind, src(peer), dst(s), peer, s).start()

    def wait_one(name, origin):
        kind, src, dst = seq_kinds[name]
        seq_copy(kind, src(origin), dst(origin), origin, origin).wait_recv()

    def each_peer(fn, me, count):
        def body(step, carry):
            fn(lax.rem(me + step, count))
            return carry
        lax.fori_loop(1, count, body, 0)

    def send_seq(name):
        each_peer(lambda p: send_one(name, p), s, n)

    def wait_seq(name):
        each_peer(lambda p: wait_one(name, p), s, n)

    def sent_seq(name):
        kind, src, dst = seq_kinds[name]
        each_peer(lambda p: seq_copy(kind, src(p), dst(s), p, s).wait_send(), s, n)

    def send_grp_one(name, peer):
        kind, src, dst = grp_kinds[name]
        grp_copy(kind, src(peer), dst(g), peer, g).start()

    def wait_grp(name):
        kind, src, dst = grp_kinds[name]
        each_peer(lambda p: grp_copy(kind, src(p), dst(p), p, p).wait_recv(), g, groups)

    def sent_grp(name):
        kind, src, dst = grp_kinds[name]
        each_peer(lambda p: grp_copy(kind, src(p), dst(g), p, g).wait_send(), g, groups)

    barrier = pltpu.get_barrier_semaphore()

    def greet_seq(p):
        pl.semaphore_signal(barrier, inc=1, device_id={"seq": p}, device_id_type=MESH)

    def greet_grp(p):
        pl.semaphore_signal(barrier, inc=1, device_id={"grp": p}, device_id_type=MESH)

    each_peer(greet_seq, s, n)
    each_peer(greet_grp, g, groups)

    own = {}
    x_parts = [("x", part) for part in range(chunks)]
    for number, name in enumerate(["k", "q", "o"] + x_parts):
        _, src, dst = seq_kinds[name]
        own[name] = pltpu.make_async_copy(src(s), dst(s), near.at[number])
    own["a"] = pltpu.make_async_copy(ad, adv, near.at[3 + chunks])
    own["b"] = pltpu.make_async_copy(au, auv, near.at[4 + chunks])
    for name in ["a", "b", "k", "q", "o"] + x_parts:
        own[name].start()

    chosen_rows(sai, row, g, sel_s, groups, segs, resident, cap)
    owners, ranks, places, _ = segment_places(sai, row, g, segs, resident, cap)
    ends = []
    total = jnp.int32(0)
    for j in range(segs):
        total = total + cnt[g, j]
        ends.append(total)
    for b in range(pad):
        seg_s[b] = jnp.int32(-1)

    def one_block(b, carry):
        seg = jnp.int32(0)
        for j in range(segs):
            seg = seg + jnp.where(b >= ends[j], 1, 0)
        place = jnp.int32(0)
        for j in range(segs):
            place = jnp.where(seg == j, places[j], place)
        seg_s[pad + b] = seg
        place_s[b] = place
        return carry

    lax.fori_loop(0, n, one_block, 0)

    def partner(step):
        index, bit = 0, 1
        while bit < n:
            ours, flip = (s // bit) % 2, (step // bit) % 2
            index = index + (ours + flip - 2 * ours * flip) * bit
            bit *= 2
        return index

    def send_heads(p):
        for name in ("q", "o"):
            send_one(name, p)

    order = [1, 2, 4, 6, 3, 5, 7] if n == 8 else list(range(1, n))
    ahead = min(4, n - 1)
    pl.semaphore_wait(barrier, n - 1 + groups - 1)
    send_seq("k")
    for step in order[:ahead]:
        send_heads(partner(step))

    own["a"].wait()
    own["b"].wait()

    def pick(slot, carry):
        index = jnp.maximum(sel_s[slot], 0)
        asend[slot] = adv[index]
        usend[slot] = auv[index]
        return carry

    lax.fori_loop(0, groups * cap, pick, 0)
    each_peer(lambda p: send_grp_one("b", p), g, groups)
    each_peer(lambda p: send_grp_one("a", p), g, groups)
    for c in range(cap):
        acand[g * cap + c] = asend[g * cap + c]
        ucand[g * cap + c] = usend[g * cap + c]
    for b in range(pad):
        kb[b] = jnp.zeros_like(kb[b])
    acc[...] = jnp.zeros_like(acc)

    def route(b, carry):
        u2send[b] = ucand[place_s[b]]
        return carry

    def route_up():
        wait_grp("b")
        lax.fori_loop(0, n, route, 0)
        send_seq("u")
        u2[s] = u2send[s]

    factor = math.log2(math.e) / math.sqrt(HEAD_DIM)

    def attend(b, first, count):
        queries = jnp.concatenate(
            [qb[b, :, h * HEAD_DIM:(h + 1) * HEAD_DIM] for h in range(hh)], 0)
        grads = jnp.concatenate(
            [ob[b, :, h * HEAD_DIM:(h + 1) * HEAD_DIM] for h in range(hh)], 0)
        own_seg = seg_s[pad + b]
        scores = []
        for j in range(count):
            part = lax.dot_general(kb[first + j], queries, (((1,), (1,)), ((), ())),
                                   preferred_element_type=F32)
            if j < count - 1:
                part = part + jnp.where(seg_s[first + j] == own_seg, F32(0), F32(-1e30))
            else:
                key = lax.broadcasted_iota(jnp.int32, (blk, hh * blk), 0)
                query = lax.broadcasted_iota(jnp.int32, (blk, hh * blk), 1) % blk
                part = jnp.where(key <= query, part, F32(-1e30))
            scores.append(part)
        highest = scores[0]
        for part in scores[1:]:
            highest = jnp.maximum(highest, part)
        highest = jnp.max(highest, axis=0, keepdims=True)
        expos = [jnp.exp2((part - highest) * factor) for part in scores]
        total = expos[0]
        for part in expos[1:]:
            total = total + part
        inverse = 1.0 / jnp.sum(total, axis=0, keepdims=True)
        for j in range(count):
            acc[first + j] += lax.dot_general(
                (expos[j] * inverse).astype(BF16), grads, (((1,), (0,)), ((), ())),
                preferred_element_type=F32)

    own["k"].wait()
    own["q"].wait()
    own["o"].wait()
    wait_seq("k")
    attend(s, s, reach)

    def visit(b):
        wait_one("q", b)
        wait_one("o", b)
        attend(b, b, reach)

    first_x = n == 8
    if n == 8:
        for number, step in enumerate(order):
            if number >= 1 and number - 1 + ahead < n - 1:
                send_heads(partner(order[number - 1 + ahead]))
            if number == 2:
                route_up()
            if number == 4:
                for other in order:
                    send_one(x_parts[0], partner(other))
            visit(partner(step))
    else:
        route_up()

        def one_step(step, carry):
            @pl.when(step + ahead < n)
            def _():
                send_heads(partner(step + ahead))

            visit(partner(step))
            return carry

        lax.fori_loop(1, n, one_step, 0)

    def finish(step, carry):
        b = partner(step)
        vgsend[b] = acc[pad + b].astype(BF16)
        send_one("vg", b)
        return carry

    lax.fori_loop(1, n, finish, 0)
    vgr[s] = acc[pad + s].astype(BF16)
    if not first_x:
        send_seq(x_parts[0])
    half = (n - 1) // 2
    for name in x_parts[1:]:
        for step in order[:half]:
            send_one(name, partner(step))

    wait_seq("u")
    for i in range(n):
        uf[i * rp:(i + 1) * rp, :] = u2[i].astype(F32)
    up_rows = uf[...].astype(BF16)
    wait_seq("vg")
    share = gs // hh
    heads = []
    for kv in range(n // share):
        if share == 1:
            heads.append(vgr[kv])
        else:
            whole = vgr[kv * share].astype(F32)
            for i in range(1, share):
                whole = whole + vgr[kv * share + i].astype(F32)
            heads.append(whole.astype(BF16))
    value_grad = jnp.concatenate(heads, 1)
    back = SCALE * lax.dot_general(up_rows, value_grad, (((1,), (1,)), ((), ())),
                                   preferred_element_type=F32)
    blr[s] = back.astype(BF16)
    send_seq("bl")

    for name in x_parts[1:]:
        for step in order[half:]:
            send_one(name, partner(step))

    wait_seq("bl")
    for c in range(cap):
        for b in range(n):
            for owner in range(groups):
                masked[owner, c * rank:(c + 1) * rank, b * blk:(b + 1) * blk] = jnp.where(
                    place_s[b] == owner * cap + c, blr[b].astype(F32), F32(0)).astype(BF16)
    mine_down = []
    for part in range(chunks):
        own["x", part].wait()
        wait_seq(("x", part))
        features = xb[part].reshape(n * blk, fc)

        def down_terms(peer):
            dsend[part, peer] = lax.dot_general(
                masked[peer], features, (((1,), (0,)), ((), ())),
                preferred_element_type=F32).astype(BF16)

        def down_send(peer):
            down_terms(peer)
            send_grp_one(("d", part), peer)

        each_peer(down_send, g, groups)
        down_terms(g)
        _, src, dst = grp_kinds["d", part]
        mine_down.append(pltpu.make_async_copy(src(g), dst(g), near.at[6 + chunks + part]))
        mine_down[-1].start()

    wait_grp("a")

    def lowered(b, carry):
        weights = acand[place_s[b]]
        total = jnp.zeros((rank, blk), F32)
        for part in range(chunks):
            total = total + lax.dot_general(
                weights[:, part * fc:(part + 1) * fc], xb[part, b], (((1,), (1,)), ((), ())),
                preferred_element_type=F32)
        lowsend[b] = total.astype(BF16)
        return carry

    lax.fori_loop(0, n, lowered, 0)
    send_seq("low")
    lowr[s] = lowsend[s]

    wait_seq("low")
    low = lowr[0].astype(F32)
    for i in range(1, n):
        low = low + lowr[i].astype(F32)
    terms = SCALE * lax.dot_general(low.astype(BF16), value_grad, (((1,), (0,)), ((), ())),
                                    preferred_element_type=F32)
    for i in range(n):
        utsend[i] = terms[i * rp:(i + 1) * rp, :].astype(BF16)
    send_seq("ut")
    utr[s] = utsend[s]
    wait_seq("ut")

    def up_terms(peer):
        for c in range(cap):
            def add(b, total):
                return total + jnp.where(place_s[b] == peer * cap + c, utr[b].astype(F32), F32(0))
            tf[c * rp:(c + 1) * rp, :] = lax.fori_loop(
                0, n, add, jnp.zeros(utr.shape[1:], F32))
        tsend[peer] = tf[...].astype(BF16)

    def up_send(peer):
        up_terms(peer)
        send_grp_one("t", peer)

    each_peer(up_send, g, groups)
    up_terms(g)
    mine_up = pltpu.make_async_copy(tsend.at[g], up_out.at[g], near.at[5 + chunks])
    mine_up.start()

    for name in seq_kinds:
        sent_seq(name)
    for name in grp_kinds:
        sent_grp(name)
    for copy in mine_down:
        copy.wait()
    mine_up.wait()
    for part in range(chunks):
        wait_grp(("d", part))
    wait_grp("t")


def spread_kernel(cfg, sel_s, down, up, down_grad, up_grad):
    groups, cap, rank, rp = cfg
    step = pl.program_id(0)
    here = down_grad.shape[0]
    def rows_of(terms, ranks):
        count = groups * cap
        slots = lax.broadcasted_iota(jnp.int32, (1, count * ranks), 1)
        target = jnp.full((1, count * ranks), -1, jnp.int32)
        for i in range(count):
            inside = (slots >= i * ranks) & (slots < (i + 1) * ranks)
            first = jnp.where(sel_s[i] < 0, -(1 << 20), (sel_s[i] - step * here) * ranks)
            target = jnp.where(inside, first + slots - i * ranks, target)
        rows = lax.broadcasted_iota(jnp.int32, (here * ranks, count * ranks), 0)
        onehot = jnp.where(rows == target, F32(1), F32(0)).astype(BF16)
        return lax.dot_general(onehot, terms, (((1,), (0,)), ((), ())), preferred_element_type=F32)

    down_grad[...] = rows_of(down[...], rank).reshape(down_grad.shape)
    up_grad[...] = rows_of(up[...], rp).reshape(up_grad.shape)


def local(x, q, k, o, ad, au, sai, cnt, row):
    groups = lax.axis_size("grp")
    n = lax.axis_size("seq")
    tokens = x.shape[0]
    fw = ad.shape[2]
    resident, rank = ad.shape[0], ad.shape[1]
    rp, vw = au.shape[1], au.shape[2]
    segs = sai.shape[1]
    cap = max(2, (segs + groups - 1) // groups)
    reach = min(16, n * tokens // (2 * BLOCK))
    heads = q.shape[1] // HEAD_DIM
    hh = heads // n
    gs = heads // (vw // HEAD_DIM)
    assert tokens == BLOCK and gs % hh == 0 and n & (n - 1) == 0
    pad = reach - 1
    chunks = 2 if fw % 256 == 0 else 1
    cfg = (n, groups, cap, segs, resident, rank, rp, fw, hh, gs, reach, pad, chunks)
    slots = groups * cap
    smem = pl.BlockSpec(memory_space=pltpu.SMEM)
    hbm = pl.BlockSpec(memory_space=pl.ANY)
    down, up, sel = pl.pallas_call(
        functools.partial(exchange_kernel, cfg),
        out_shape=(
            jax.ShapeDtypeStruct((groups, cap * rank, fw), BF16),
            jax.ShapeDtypeStruct((groups, cap * rp, vw), BF16),
            jax.ShapeDtypeStruct((slots,), jnp.int32),
        ),
        in_specs=[smem] * 3 + [pl.BlockSpec(memory_space=pltpu.HBM)] * 6,
        out_specs=(hbm, hbm, smem),
        scratch_shapes=[
            pltpu.SMEM((n + pad,), jnp.int32),
            pltpu.SMEM((n,), jnp.int32),
            pltpu.VMEM((n, BLOCK, hh * HEAD_DIM), BF16),
            pltpu.VMEM((n, BLOCK, hh * HEAD_DIM), BF16),
            pltpu.VMEM((n + pad, BLOCK, HEAD_DIM), BF16),
            pltpu.VMEM((chunks, n, BLOCK, fw // chunks), BF16),
            pltpu.VMEM(ad.shape, BF16),
            pltpu.VMEM(au.shape, BF16),
            pltpu.VMEM((slots, rank, fw), BF16),
            pltpu.VMEM((slots, rp, vw), BF16),
            pltpu.VMEM((slots, rank, fw), BF16),
            pltpu.VMEM((slots, rp, vw), BF16),
            pltpu.VMEM((n, rp, vw), BF16),
            pltpu.VMEM((n, rp, vw), BF16),
            pltpu.VMEM((rank, vw), F32),
            pltpu.VMEM((n, rank, BLOCK), BF16),
            pltpu.VMEM((n, rank, BLOCK), BF16),
            pltpu.VMEM((n, BLOCK, HEAD_DIM), BF16),
            pltpu.VMEM((n, BLOCK, HEAD_DIM), BF16),
            pltpu.VMEM((n, rank, BLOCK), BF16),
            pltpu.VMEM((n, rp, vw), BF16),
            pltpu.VMEM((n, rp, vw), BF16),
            pltpu.VMEM((groups, cap * rank, n * BLOCK), BF16),
            pltpu.VMEM((chunks, groups, cap * rank, fw // chunks), BF16),
            pltpu.VMEM((cap * rp, vw), F32),
            pltpu.VMEM((groups, cap * rp, vw), BF16),
            pltpu.VMEM((n + pad, BLOCK, HEAD_DIM), F32),
            pltpu.SemaphoreType.DMA((8 + chunks, n)),
            pltpu.SemaphoreType.DMA((8 + chunks, n)),
            pltpu.SemaphoreType.DMA((3 + chunks, groups)),
            pltpu.SemaphoreType.DMA((3 + chunks, groups)),
            pltpu.SemaphoreType.DMA((6 + 2 * chunks,)),
        ],
        compiler_params=pltpu.CompilerParams(
            collective_id=0, has_side_effects=True, vmem_limit_bytes=60 * 1024 * 1024),
        name="exchange",
    )(sai, cnt, row, x, q, k, o, ad, au)
    steps = 4
    here = resident // steps
    return pl.pallas_call(
        functools.partial(spread_kernel, (groups, cap, rank, rp)),
        grid=(steps,),
        out_shape=(
            jax.ShapeDtypeStruct((resident, rank, fw), F32),
            jax.ShapeDtypeStruct((resident, rp, vw), F32),
        ),
        in_specs=[
            smem,
            pl.BlockSpec((slots * rank, fw), lambda i: (0, 0)),
            pl.BlockSpec((slots * rp, vw), lambda i: (0, 0)),
        ],
        out_specs=(
            pl.BlockSpec((here, rank, fw), lambda i: (i, 0, 0)),
            pl.BlockSpec((here, rp, vw), lambda i: (i, 0, 0)),
        ),
        compiler_params=pltpu.CompilerParams(vmem_limit_bytes=60 * 1024 * 1024),
        name="spread",
    )(sel, down.reshape(slots * rank, fw), up.reshape(slots * rp, vw))


def solution(mesh):
    return jax.shard_map(
        local,
        mesh=mesh,
        in_specs=(
            P(("grp", "seq"), None),
            P(("grp", "seq"), None),
            P(("grp", "seq"), None),
            P(("grp", "seq"), None),
            P("grp", None, "seq"),
            P("grp", "seq", None),
            P(),
            P(),
            P(),
        ),
        out_specs=(P("grp", None, "seq"), P("grp", "seq", None)),
        check_vma=False,
    )
```
